512 devices in a mesh: expert: 128 (over y, z, core), half: 4 (over x).
Axes of the slice: x: 4, y: 4, z: 16, core: 2. Of those that a mesh axis runs over, the one named last changes fastest.
Arguments:
- tokens: bfloat16 [2048, 2048], P('expert', 'half'), may hold values from -6 to 6
- upstream: bfloat16 [2048, 2048], P('expert', 'half'), may hold values from -6 to 6
- expert_ids: int32 [2048, 8], P('expert'), may hold values from 0 to 127, all different within a row; in each aligned block of 16 rows (0 to 15, 16 to 31, ...) at most 2 rows name the same one
- gate_probs: float32 [2048, 8], P('expert'), may hold values from 0.01 to 1
- pad_mask: int32 [2048], P('expert'), may hold values 0 or 1
- gate_weight: bfloat16 [128, 2048, 1536], P('expert', None, 'half'), may hold values from -0.125 to 0.125
- up_weight: bfloat16 [128, 2048, 1536], P('expert', None, 'half'), may hold values from -0.125 to 0.125
- down_weight: bfloat16 [128, 1536, 2048], P('expert', 'half'), may hold values from -0.15625 to 0.15625
Outputs:
- layer_out: bfloat16 [2048, 2048], P('expert', 'half')
- grad_tokens: bfloat16 [2048, 2048], P('expert', 'half')
The draws below stay inside these ranges and needn't reach their ends.
Inputs may be any that keep to these rules, and one draw needn't show every extreme that they name: `expert_ids`: each row names 8 different experts. In the rows of one device (aligned blocks of 16 rows) no expert is named more than 2 times, a bound that some block reaches.
All inputs are finite; a program needn't handle non-finite values. No bound on the sum of `pad_mask` on one device may be relied on, other than what follows from the above.
Results may differ from the reference program's by a relative error of at most 0.025.
Values may be sent and summed in bfloat16 or wider, within the bound.
No kernel may reach another device: no remote copies, remote signals or barrier semaphores. Data moves between devices by JAX's collectives and lax.ppermute only.
A program may use at most 64 MiB of HBM per device.

```python
import math
import jax
import jax.numpy as jnp
import numpy as np
from jax import lax

D = 2048
HID = 1536
TOPK = 8
TOK_DEV = 16
EXPERTS = 128
CAP = 2
TOKENS = 2048
N_EXPERT = 128
N_HALF = 4


def touch_ends(entries, rng, least, high):
    longest = entries.shape.index(max(entries.shape))
    spots = []
    for shift in (0, 1):
        where = [jax.random.randint(jax.random.fold_in(rng, axis), (), 0, length) for axis, length in enumerate(entries.shape)]
        where[longest] = (where[longest] + shift) % entries.shape[longest]
        spots.append(tuple(where))
    return entries.at[spots[0]].set(least).at[spots[1]].set(high)


def shard_levels(rng, shape, split, least, high):
    level, own = 1.0, jax.random.fold_in(rng, 6)
    for dim, shards_of in split:
        heights = jnp.exp(jax.random.uniform(jax.random.fold_in(own, dim), (shards_of,), jnp.float32, least / len(split), high / len(split)))
        level = level * jnp.repeat(heights, shape[dim] // shards_of).reshape([-1 if axis == dim else 1 for axis in range(len(shape))])
    return level


def shared_out(key, own, number, rows, count, top, most, slope):
    sequence = jax.random.permutation(key, count)
    heavy_load, usual = portions_of(count, rows * top, most, slope, True), portions_of(count, rows * top, most, slope, False)
    places = jnp.arange(count)

    def named(lengths, offset_by):
        used = int((lengths > 0).sum())
        fixed = max(1, used // 4)
        moved = fixed + (places - fixed + offset_by * (used - fixed)) % max(1, count - fixed)
        return jnp.zeros((count,), jnp.int32).at[sequence[jnp.where(places < fixed, places, moved)]].set(jnp.asarray(lengths, jnp.int32))

    lengths = jnp.where(number % 4 == 0, named(heavy_load, number // 4), named(usual, number - number // 4 - 1))
    mixed = jax.random.permutation(jax.random.fold_in(own, 3), count)
    source_of, sink = mixed[0:count // 2 * 2:2], mixed[1:count // 2 * 2:2]
    margin = jnp.minimum(lengths[source_of] - 1, most - lengths[sink]) // 2
    margin = jnp.where((source_of == sequence[0]) | (sink == sequence[0]) | (lengths[sink] == 0), 0, jnp.maximum(margin, 0))
    moved = jax.random.randint(jax.random.fold_in(own, 4), (count // 2,), 0, 1 << 20) % (margin + 1)
    lengths = lengths.at[source_of].add(-moved).at[sink].add(moved)
    items = jnp.searchsorted(jnp.cumsum(lengths), jnp.arange(rows * top), side="right").astype(jnp.int32)
    listing = items.reshape(top, rows).T
    listing = listing[jax.random.permutation(jax.random.fold_in(own, 1), rows)]
    offset_by = jax.random.randint(jax.random.fold_in(own, 2), (rows, 1), 0, top)
    return jnp.take_along_axis(listing, (jnp.arange(top)[None, :] + offset_by) % top, axis=1)


def portions_of(count, total, reach, skew, full):
    weights = [(1 << 20) // math.isqrt(rank ** skew) + 1 for rank in range(1, count + 1)]
    largest = reach if full else min(reach, max(-(-total // count), total * weights[0] // sum(weights)))
    least = 1 if total - largest >= count - 1 else 0
    counts, surplus = [largest] + [least] * (count - 1), total - largest - least * (count - 1)
    while surplus > 0:
        movable = [i for i in range(1, count) if counts[i] < largest] or [i for i in range(1, count) if counts[i] < reach]
        pool, budget = sum([weights[i] for i in movable]), surplus
        for i in movable:
            extra = min(reach - counts[i], max(1, budget * weights[i] // pool), surplus)
            counts[i] = counts[i] + extra
            surplus = surplus - extra
    return np.array(counts)


def noise(key, extent, scale, bound, shards=(), kind=jnp.bfloat16):
    drawn = jax.random.normal(key, extent, jnp.float32) * scale
    if len(shards) > 0:
        drawn = shard_levels(key, extent, shards, -0.22, 0.18) * drawn
    return jnp.clip(drawn, min=-bound, max=bound).astype(kind)


def setup_inputs(seed: int = 0) -> dict:
    key_of = jax.random.split(jax.random.key(seed), 9)
    tokens = noise(key_of[0], (TOKENS, D), 1.0, 6.0, ((0, 128), (1, 4)))
    upstream = noise(key_of[1], (TOKENS, D), 1.0, 6.0, ((0, 128), (1, 4)))
    expert_ids_keys = jax.random.split(jax.random.fold_in(key_of[2], 1), TOKENS // TOK_DEV)
    expert_ids_turns = jax.random.permutation(jax.random.fold_in(key_of[2], 3), TOKENS // TOK_DEV)
    expert_ids = jax.vmap(lambda own, number: shared_out(jax.random.fold_in(key_of[2], 2), own, number, TOK_DEV, EXPERTS, TOPK, CAP, 2))(expert_ids_keys, expert_ids_turns).reshape((TOKENS, TOPK))
    gate_probs = jnp.clip(jnp.exp(math.log(1.0) - 4.6051702 * jax.random.uniform(key_of[3], (TOKENS, TOPK), jnp.float32) ** shard_levels(key_of[3], (TOKENS, TOPK), ((0, 128),), -0.2, 0.2)), 0.01, 1.0)
    pad_mask = touch_ends((jax.random.randint(key_of[4], (TOKENS,), 0, 8) < 7).astype(jnp.int32), jax.random.fold_in(key_of[4], 1), 0, 1)
    gate_weight = noise(key_of[5], (EXPERTS, D, HID), D ** -0.5, 0.125, ((0, 128), (2, 4)))
    up_weight = noise(key_of[6], (EXPERTS, D, HID), D ** -0.5, 0.125, ((0, 128), (2, 4)))
    down_weight = noise(key_of[7], (EXPERTS, HID, D), HID ** -0.5, 0.15625, ((0, 128), (1, 4)))
    return {"tokens": tokens, "upstream": upstream, "expert_ids": expert_ids, "gate_probs": gate_probs, "pad_mask": pad_mask, "gate_weight": gate_weight, "up_weight": up_weight, "down_weight": down_weight}


orth_weight = 0.25

def slot_numbers(expert_ids):
    blocks = expert_ids.reshape(N_EXPERT, TOK_DEV * TOPK)
    onehot = (blocks[:, :, None] == jnp.arange(EXPERTS, dtype=jnp.int32)[None, None, :]).astype(jnp.int32)
    before = jnp.cumsum(onehot, axis=1) - onehot
    slot_index = lax.optimization_barrier(jnp.sum(before * onehot, axis=2))
    return slot_index.reshape(TOKENS * TOPK).astype(jnp.int32)

def rounded(value):
    return lax.optimization_barrier(value.astype(jnp.bfloat16)).astype(jnp.float32)

def reference(tokens, upstream, expert_ids, gate_probs, pad_mask, gate_weight, up_weight, down_weight):
    piece_width = HID // N_HALF
    slot_index = slot_numbers(expert_ids)
    flat_ids = expert_ids.reshape(TOKENS * TOPK).astype(jnp.int32)
    item_index = jnp.arange(TOKENS * TOPK, dtype=jnp.int32)
    source = item_index // (TOK_DEV * TOPK)
    table = jnp.full((EXPERTS, N_EXPERT * CAP), -1, jnp.int32)
    table = table.at[flat_ids, source * CAP + slot_index].set(item_index)

    def expert_inputs(row_ids):
        valid = row_ids >= 0
        safe = jnp.where(valid, row_ids, 0)
        rows_in = jnp.where(valid[:, None], tokens[safe // TOPK], jnp.zeros((), jnp.bfloat16))
        return (valid, safe, rows_in)

    def forward(carry, packed):
        row_ids, weight_gate, weight_up, weight_down = packed
        valid, safe, rows_in = expert_inputs(row_ids)
        gate_val = jnp.dot(rows_in, weight_gate, preferred_element_type=jnp.float32)
        up_val = jnp.dot(rows_in, weight_up, preferred_element_type=jnp.float32)
        hidden_act = (jax.nn.silu(gate_val) * up_val).astype(jnp.bfloat16)
        total = jnp.zeros((N_EXPERT * CAP, D), jnp.float32)
        for piece in range(N_HALF):
            lower = piece * piece_width
            term = jnp.dot(hidden_act[:, lower:lower + piece_width], weight_down[lower:lower + piece_width], preferred_element_type=jnp.float32)
            total = total + rounded(term)
        out_rows = total.astype(jnp.bfloat16)
        target = jnp.where(valid, safe, TOKENS * TOPK)
        carry = carry.at[target].set(out_rows, mode='drop')
        return (carry, None)
    outputs, _ = lax.scan(forward, jnp.zeros((TOKENS * TOPK, D), jnp.bfloat16), (table, gate_weight, up_weight, down_weight))
    out_float = outputs.reshape(TOKENS, TOPK, D).astype(jnp.float32)
    shares = gate_probs / lax.optimization_barrier(jnp.sum(gate_probs, axis=1, keepdims=True))
    layer_out = lax.optimization_barrier(jnp.sum(shares[:, :, None] * out_float, axis=1)).astype(jnp.bfloat16)
    gram = jnp.einsum('tjd,tkd->tjk', out_float, out_float) / jnp.sqrt(jnp.float32(D))
    off_diag = 1.0 - jnp.eye(TOPK, dtype=jnp.float32)
    coeffs = orth_weight * gram * off_diag
    grad_out = pad_mask.astype(jnp.float32)[:, None, None] * (shares[:, :, None] * upstream.astype(jnp.float32)[:, None, :] + jnp.einsum('tjk,tkd->tjd', coeffs, out_float))
    grad_items = grad_out.astype(jnp.bfloat16).reshape(TOKENS * TOPK, D)

    def backward(carry, packed):
        row_ids, weight_gate, weight_up, weight_down = packed
        valid, safe, rows_in = expert_inputs(row_ids)
        gate_val = jnp.dot(rows_in, weight_gate, preferred_element_type=jnp.float32)
        up_val = jnp.dot(rows_in, weight_up, preferred_element_type=jnp.float32)
        grad_rows = jnp.where(valid[:, None], grad_items[safe], jnp.zeros((), jnp.bfloat16))
        grad_act = jnp.dot(grad_rows, weight_down.T, preferred_element_type=jnp.float32)
        sigma = jax.nn.sigmoid(gate_val)
        grad_gate = (grad_act * up_val * sigma * (1.0 + gate_val * (1.0 - sigma))).astype(jnp.bfloat16)
        grad_up = (grad_act * gate_val * sigma).astype(jnp.bfloat16)
        total = jnp.zeros((N_EXPERT * CAP, D), jnp.float32)
        for piece in range(N_HALF):
            lower = piece * piece_width
            term = jnp.dot(grad_gate[:, lower:lower + piece_width], weight_gate[:, lower:lower + piece_width].T, preferred_element_type=jnp.float32)
            term = term + jnp.dot(grad_up[:, lower:lower + piece_width], weight_up[:, lower:lower + piece_width].T, preferred_element_type=jnp.float32)
            total = total + rounded(term)
        grad_in_rows = total.astype(jnp.bfloat16).astype(jnp.float32)
        target = jnp.where(valid, safe // TOPK, TOKENS)
        carry = carry.at[target].add(grad_in_rows, mode='drop')
        return (carry, None)
    grad_sum, _ = lax.scan(backward, jnp.zeros((TOKENS, D), jnp.float32), (table, gate_weight, up_weight, down_weight))
    return (layer_out, grad_sum.astype(jnp.bfloat16))
```

```python
import math

import jax
import jax.numpy as jnp
from jax import lax
from jax.experimental import pallas as pl
from jax.experimental.pallas import tpu as pltpu
from jax.sharding import Mesh
from jax.sharding import PartitionSpec as P

orth_weight = 0.25
NY, NZ, NC, NH = 4, 16, 2, 4
TOK, TOPK, WIDE, PART = 16, 8, 2048, 512
PAIRS = TOK * TOPK
ROWS = 256
F32, BF16 = jnp.float32, jnp.bfloat16
HIGHEST = lax.Precision.HIGHEST


def iota(shape, dim):
    return lax.broadcasted_iota(jnp.int32, shape, dim)


def one_hot(where):
    return jnp.where(where, 1.0, 0.0).astype(BF16)


def dot(a, b, dims=((1,), (0,)), precision=None):
    return lax.dot_general(a, b, (dims, ((), ())), precision=precision, preferred_element_type=F32)


def call(body, outs, *operands, vmem=32 << 20):
    specs = [pl.BlockSpec(memory_space=pltpu.SMEM if o.ndim == 1 else pltpu.VMEM) for o in operands]
    return pl.pallas_call(
        body,
        out_shape=[jax.ShapeDtypeStruct(shape, kind) for shape, kind in outs],
        in_specs=specs,
        out_specs=[pl.BlockSpec(memory_space=pltpu.VMEM) for _ in outs],
        compiler_params=pltpu.CompilerParams(vmem_limit_bytes=vmem),
    )(*operands)


def select_body(z_ref, a_ref, out_ref):
    every = a_ref[...].reshape(NZ * TOK, PART + 128)
    named = dot(one_hot(iota((TOPK, 128), 0) == iota((TOPK, 128), 1)), every[:, PART:], ((1,), (1,)))
    row, lane = iota((ROWS, 1), 0), iota((1, ROWS), 1)
    expert = (((row >> 6) * NZ + z_ref[0]) * NC + ((row >> 5) & 1)).astype(F32)
    found = named[0:1, :] == expert
    for k in range(1, TOPK):
        found = found | (named[k : k + 1, :] == expert)
    found = found & (((row >> 1) & 15) == (lane >> 4))
    left, right = iota((ROWS, ROWS), 0), iota((ROWS, ROWS), 1)
    earlier = one_hot(((left >> 4) == (right >> 4)) & (left < right))
    rank = dot(one_hot(found), earlier)
    pick = one_hot(found & (rank == (row & 1).astype(F32)))
    chosen = dot(pick, every[:, :PART]).astype(BF16).reshape(NY * NC, 32, PART)
    for h in range(NH):
        out_ref[:, h] = chosen


def home_body(ids_ref, probs_ref, up_ref, pm_ref, share_ref, su_ref, mask_ref):
    pair, lane = iota((PAIRS, 1), 0), iota((1, PAIRS), 1)
    repeat = one_hot((iota((PAIRS, TOK), 0) >> 3) == iota((PAIRS, TOK), 1))
    ids = ids_ref[...].astype(BF16)
    tall = dot(repeat, ids)
    col = iota((PAIRS, 16), 1)
    ids_col = jnp.sum(jnp.where(col == (pair & 7), tall, 0.0), axis=1, keepdims=True)
    pad_col = jnp.sum(jnp.where(col == 8, tall, 0.0), axis=1, keepdims=True)
    flat = dot(ids, repeat, ((0,), (1,)))
    ids_row = jnp.sum(jnp.where(iota((16, PAIRS), 0) == (lane & 7), flat, 0.0), axis=0, keepdims=True)
    before = (ids_col == ids_row) & ((lane >> 3) < (pair >> 3))
    slot = jnp.sum(jnp.where(before, 1.0, 0.0), axis=1, keepdims=True)
    row = iota((1, ROWS), 1)
    expert = ((((row >> 2) & 3) * NZ + (row >> 4)) * NC + ((row >> 1) & 1)).astype(F32)
    pm_ref[...] = one_hot((expert == ids_col) & ((row & 1).astype(F32) == slot))
    probs = probs_ref[...]
    shares = probs / jnp.sum(probs, axis=1, keepdims=True)
    wide = repeat.astype(F32)
    share_tall = dot(wide, shares, precision=HIGHEST)
    share_col = jnp.sum(jnp.where(iota((PAIRS, TOPK), 1) == (pair & 7), share_tall, 0.0), axis=1, keepdims=True)
    share_flat = dot(shares, wide, ((0,), (1,)), precision=HIGHEST)
    share_row = jnp.sum(jnp.where(iota((TOPK, PAIRS), 0) == (lane & 7), share_flat, 0.0), axis=0, keepdims=True)
    share_ref[...] = jnp.where(iota((TOK, PAIRS), 0) == (iota((TOK, PAIRS), 1) >> 3), share_row, 0.0)
    su_ref[...] = (pad_col * share_col) * dot(repeat, up_ref[...])
    same = ((lane >> 3) == (pair >> 3)) & (lane != pair)
    mask_ref[...] = jnp.where(same, pad_col * (orth_weight / math.sqrt(WIDE)), 0.0)


def forward_body(x_ref, wg_ref, wu_ref, wd_ref, out_ref, dgate_ref, dup_ref):
    gate = up = None
    for h in range(NH):
        x = x_ref[:, h].reshape(ROWS, PART)
        g = dot(x, wg_ref[h * PART : (h + 1) * PART, :])
        u = dot(x, wu_ref[h * PART : (h + 1) * PART, :])
        gate, up = (g, u) if gate is None else (gate + g, up + u)
    sigma = 1.0 / (1.0 + jnp.exp(-gate))
    act = gate * sigma
    hidden = (act * up).astype(BF16)
    for h in range(NH):
        part = dot(hidden, wd_ref[:, h * PART : (h + 1) * PART])
        out_ref[:, h] = part.astype(BF16).reshape(NY * NC, 32, PART)
    dup_ref[...] = act
    dgate_ref[...] = up * sigma * (1.0 + gate * (1.0 - sigma))


def backward_body(g_ref, wg_ref, wu_ref, wd_ref, dgate_ref, dup_ref, out_ref):
    act = None
    for h in range(NH):
        a = dot(g_ref[:, h].reshape(ROWS, PART), wd_ref[:, h * PART : (h + 1) * PART], ((1,), (1,)))
        act = a if act is None else act + a
    gate = (act * dgate_ref[...]).astype(BF16)
    up = (act * dup_ref[...]).astype(BF16)
    for h in range(NH):
        part = dot(gate, wg_ref[h * PART : (h + 1) * PART, :], ((1,), (1,)))
        part = part + dot(up, wu_ref[h * PART : (h + 1) * PART, :], ((1,), (1,)))
        out_ref[:, h] = part.astype(BF16).reshape(NY * NC, 32, PART)


def reduce_body(p_ref, out_ref):
    total = p_ref[:, 0].astype(F32)
    for h in range(1, NH):
        total = total + p_ref[:, h].astype(F32)
    row, lane = iota((ROWS, ROWS), 0), iota((ROWS, ROWS), 1)
    order = one_hot(lane == ((row >> 1) & 7) * 32 + (row >> 4) * 2 + (row & 1))
    moved = dot(order, total.astype(BF16).reshape(ROWS, PART)).astype(BF16)
    out_ref[...] = moved.reshape(NZ, 16, PART)


def spread_body(r_ref, out_ref):
    row, lane = iota((ROWS, ROWS), 0), iota((ROWS, ROWS), 1)
    order = one_hot(lane == ((row >> 1) & 15) * 16 + (row >> 5) * 2 + (row & 1))
    moved = dot(order, r_ref[...].reshape(ROWS, PART)).astype(BF16).reshape(NY * NC, 32, PART)
    for h in range(NH):
        out_ref[:, h] = moved


def gram_body(r_ref, pm_ref, share_ref, out_ref, gram_ref, layer_ref):
    out = dot(pm_ref[...], r_ref[...].reshape(ROWS, PART)).astype(BF16)
    full = dot(out, out, ((1,), (1,)))
    full = jnp.where((iota((PAIRS, PAIRS), 0) >> 3) == (iota((PAIRS, PAIRS), 1) >> 3), full, 0.0)
    packed = jnp.sum(full.reshape(TOK, TOPK, PAIRS), axis=0)
    for h in range(NH):
        gram_ref[h] = packed
    out_ref[...] = out
    layer_ref[...] = dot(share_ref[...], out.astype(F32), precision=HIGHEST).astype(BF16)


def grad_body(gram_ref, out_ref, su_ref, mask_ref, pm_ref, rows_ref):
    packed = (gram_ref[0] + gram_ref[1]) + (gram_ref[2] + gram_ref[3])
    full = jnp.broadcast_to(packed[None], (TOK, TOPK, PAIRS)).reshape(PAIRS, PAIRS)
    grad = su_ref[...] + dot(full * mask_ref[...], out_ref[...].astype(F32), precision=HIGHEST)
    rows = dot(pm_ref[...], grad.astype(BF16), ((0,), (0,))).astype(BF16)
    rows_ref[...] = rows.reshape(NZ, 16, PART)


def combine_body(r_ref, pm_ref, out_ref):
    repeat = one_hot(iota((TOK, PAIRS), 0) == (iota((TOK, PAIRS), 1) >> 3))
    pick = dot(repeat, pm_ref[...]).astype(BF16)
    out_ref[...] = dot(pick, r_ref[...].reshape(ROWS, PART)).astype(BF16)


def over_z(x):
    return lax.all_to_all(x, "z", 0, 0, tiled=True)


def over_plane(x):
    shape = x.shape
    x = lax.all_to_all(x.reshape(NY * NC * NH, 32, PART), ("y", "c", "h"), 0, 0, tiled=True)
    return x.reshape(shape)


def shards(tokens, upstream, expert_ids, gate_probs, pad_mask, gate_weight, up_weight, down_weight):
    wg, wu, wd = gate_weight[0], up_weight[0], down_weight[0]
    tagged = jnp.concatenate([tokens, jnp.pad(expert_ids.astype(BF16), ((0, 0), (0, 128 - TOPK)))], axis=1)
    every = over_z(jnp.broadcast_to(tagged[None], (NZ, TOK, PART + 128)))
    packed_ids = jnp.concatenate([expert_ids, pad_mask[:, None], jnp.zeros((TOK, 7), jnp.int32)], axis=1).astype(F32)
    pm, share, su, mask = call(
        home_body,
        [((PAIRS, ROWS), BF16), ((TOK, PAIRS), F32), ((PAIRS, PART), F32), ((PAIRS, PAIRS), F32)],
        packed_ids, gate_probs, upstream,
    )
    plane = ((NY * NC, NH, 32, PART), BF16)
    ring = ((NZ, 16, PART), BF16)
    hidden = ((ROWS, wg.shape[1]), F32)
    (picked,) = call(select_body, [plane], lax.axis_index("z").astype(jnp.int32).reshape(1), every)
    rows_in = over_plane(picked)
    partial, dgate, dup = call(forward_body, [plane, hidden, hidden], rows_in, wg, wu, wd)
    (summed,) = call(reduce_body, [ring], over_plane(partial))
    out, gram, layer_out = call(
        gram_body,
        [((PAIRS, PART), BF16), ((NH, TOPK, PAIRS), F32), ((TOK, PART), BF16)],
        over_z(summed), pm, share,
    )
    gram = lax.all_to_all(gram, "h", 0, 0, tiled=True)
    (grad_rows,) = call(grad_body, [ring], gram, out, su, mask, pm)
    (spread,) = call(spread_body, [plane], over_z(grad_rows))
    (partial,) = call(backward_body, [plane], over_plane(spread), wg, wu, wd, dgate, dup)
    (summed,) = call(reduce_body, [ring], over_plane(partial))
    (grad_tokens,) = call(combine_body, [((TOK, PART), BF16)], over_z(summed), pm)
    return (layer_out, grad_tokens)


def solution(mesh):
    fine = Mesh(mesh.devices.reshape(NY, NZ, NC, NH), ("y", "z", "c", "h"))
    expert = ("y", "z", "c")
    in_specs = (
        P(expert, "h"),
        P(expert, "h"),
        P(expert, None),
        P(expert, None),
        P(expert),
        P(expert, None, "h"),
        P(expert, None, "h"),
        P(expert, "h", None),
    )
    return jax.shard_map(shards, mesh=fine, in_specs=in_specs, out_specs=(P(expert, "h"), P(expert, "h")), check_vma=False)
```

```python
import math

import jax
import jax.numpy as jnp
from jax import lax
from jax.experimental import pallas as pl
from jax.experimental.pallas import tpu as pltpu
from jax.sharding import Mesh
from jax.sharding import PartitionSpec as P

orth_weight = 0.25
NY, NZ, NC, NH = 4, 16, 2, 4
TOK, TOPK, WIDE, PART = 16, 8, 2048, 512
PAIRS = TOK * TOPK
ROWS, HALF = 256, 128
F32, BF16 = jnp.float32, jnp.bfloat16
HIGHEST = lax.Precision.HIGHEST


def iota(shape, dim):
    return lax.broadcasted_iota(jnp.int32, shape, dim)


def one_hot(where):
    return jnp.where(where, 1.0, 0.0).astype(BF16)


def dot(a, b, dims=((1,), (0,)), precision=None):
    return lax.dot_general(a, b, (dims, ((), ())), precision=precision, preferred_element_type=F32)


def call(body, outs, *operands, vmem=8 << 20, space=None, remote=(), scratch=(), cost=None):
    specs = [pl.BlockSpec(memory_space=pltpu.SMEM if o.ndim == 1 else pltpu.VMEM) for o in operands]
    specs += [pl.BlockSpec(memory_space=pltpu.HBM) for _ in remote]
    return pl.pallas_call(
        body,
        out_shape=[(space or jax.ShapeDtypeStruct)(shape, kind) for shape, kind in outs],
        in_specs=specs,
        out_specs=[pl.BlockSpec(memory_space=pltpu.VMEM) for _ in outs],
        scratch_shapes=scratch,
        cost_estimate=cost,
        compiler_params=pltpu.CompilerParams(vmem_limit_bytes=vmem),
    )(*operands, *(pltpu.with_memory_space_constraint(r, pltpu.HBM) for r in remote))


def fetch(pairs, sems):
    copies = [pltpu.make_async_copy(src, dst, sems.at[i]) for i, (src, dst) in enumerate(pairs)]
    for c in copies:
        c.start()
    for c in copies:
        c.wait()


def pack_body(tok_hbm, ids_hbm, out_ref, tok_ref, ids_ref, sems):
    fetch([(tok_hbm, tok_ref), (ids_hbm, ids_ref)], sems)
    place = one_hot(iota((TOPK, 128), 0) == iota((TOPK, 128), 1))
    ids = dot(ids_ref[...].astype(F32).astype(BF16), place, ((0,), (0,))).astype(BF16)
    row = jnp.concatenate([tok_ref[...], ids], axis=1)
    for z in range(NZ):
        out_ref[z] = row


def select_body(where_ref, a_ref, out_ref):
    every = a_ref[...].reshape(NZ * TOK, PART + 128)
    named = dot(one_hot(iota((TOPK, 128), 0) == iota((TOPK, 128), 1)), every[:, PART:], ((1,), (1,)))
    row, lane = iota((ROWS, 1), 0), iota((1, ROWS), 1)
    expert = (((row >> 6) * NZ + where_ref[0]) * NC + (((row >> 5) + where_ref[1]) & 1)).astype(F32)
    found = named[0:1, :] == expert
    for k in range(1, TOPK):
        found = found | (named[k : k + 1, :] == expert)
    found = found & (((row >> 1) & 15) == (lane >> 4))
    left, right = iota((ROWS, ROWS), 0), iota((ROWS, ROWS), 1)
    earlier = one_hot(((left >> 4) == (right >> 4)) & (left < right))
    rank = dot(one_hot(found), earlier)
    pick = one_hot(found & (rank == (row & 1).astype(F32)))
    chosen = dot(pick, every[:, :PART]).astype(BF16).reshape(NY, 64, PART)
    for h in range(NH):
        out_ref[:, h] = chosen


def home_body(where_ref, ids_ref, probs_ref, pad_ref, up_ref, pm_ref, share_ref, su_ref, mask_ref):
    pair, lane = iota((PAIRS, 1), 0), iota((1, PAIRS), 1)
    owner = (iota((PAIRS, TOK), 0) >> 3) == iota((PAIRS, TOK), 1)
    repeat = one_hot(owner)
    ids = ids_ref[...].astype(F32).astype(BF16)
    tall = dot(repeat, ids, ((1,), (1,)))
    mine = iota((PAIRS, TOPK), 1) == (pair & 7)
    ids_col = jnp.sum(jnp.where(mine, tall, 0.0), axis=1, keepdims=True)
    pad_col = jnp.sum(jnp.where(owner, pad_ref[...].astype(F32), 0.0), axis=1, keepdims=True)
    flat = dot(ids, repeat, ((1,), (1,)))
    mine_row = iota((TOPK, PAIRS), 0) == (lane & 7)
    ids_row = jnp.sum(jnp.where(mine_row, flat, 0.0), axis=0, keepdims=True)
    before = (ids_col == ids_row) & ((lane >> 3) < (pair >> 3))
    slot = jnp.sum(jnp.where(before, 1.0, 0.0), axis=1, keepdims=True)
    row = iota((1, ROWS), 1)
    expert = ((((row >> 2) & 3) * NZ + (row >> 4)) * NC + (((row >> 1) + where_ref[1]) & 1)).astype(F32)
    pm_ref[...] = one_hot((expert == ids_col) & ((row & 1).astype(F32) == slot))
    probs = probs_ref[...]
    shares = probs / jnp.sum(probs, axis=0, keepdims=True)
    wide = repeat.astype(F32)
    share_tall = dot(wide, shares, ((1,), (1,)), HIGHEST)
    share_col = jnp.sum(jnp.where(mine, share_tall, 0.0), axis=1, keepdims=True)
    share_flat = dot(shares, wide, ((1,), (1,)), HIGHEST)
    share_row = jnp.sum(jnp.where(mine_row, share_flat, 0.0), axis=0, keepdims=True)
    share_ref[...] = jnp.where(iota((TOK, PAIRS), 0) == (iota((TOK, PAIRS), 1) >> 3), share_row, 0.0)
    su_ref[...] = (pad_col * share_col) * dot(repeat, up_ref[...])
    same = ((lane >> 3) == (pair >> 3)) & (lane != pair)
    mask_ref[...] = jnp.where(same, pad_col * (orth_weight / math.sqrt(WIDE)), 0.0)


def forward_body(x_ref, wg_ref, wu_ref, *refs):
    hbm, (out_ref, dgate_ref, dup_ref), held, sems = refs[:4], refs[4:7], refs[7:11], refs[11]
    copies = [pltpu.make_async_copy(src, dst, sems.at[i]) for i, (src, dst) in enumerate(zip(hbm, held))]
    for c in copies:
        c.start()
    for b, (hg, hu, hd) in enumerate(((wg_ref, wu_ref, held[0]), held[1:])):
        if b:
            copies[1].wait()
            copies[2].wait()
        gate = up = None
        for h in range(NH):
            x = x_ref[:, h, b * 32 : b * 32 + 32].reshape(HALF, PART)
            g = dot(x, hg[h * PART : (h + 1) * PART, :])
            u = dot(x, hu[h * PART : (h + 1) * PART, :])
            gate, up = (g, u) if gate is None else (gate + g, up + u)
        sigma = 1.0 / (1.0 + jnp.exp(-gate))
        act = gate * sigma
        hidden = (act * up).astype(BF16)
        dup_ref[b] = act
        dgate_ref[b] = up * sigma * (1.0 + gate * (1.0 - sigma))
        copies[3 if b else 0].wait()
        for h in range(NH):
            part = dot(hidden, hd[:, h * PART : (h + 1) * PART])
            out_ref[:, h, b * 32 : b * 32 + 32] = part.astype(BF16).reshape(NY, 32, PART)


def backward_body(g_ref, dgate_ref, dup_ref, wg_ref, wu_ref, wd_ref, *refs):
    hbm, out_ref, held, sems = refs[:3], refs[3], refs[4:7], refs[7]
    copies = [pltpu.make_async_copy(src, dst, sems.at[i]) for i, (src, dst) in enumerate(zip(hbm, held))]
    for c in (copies[2], copies[0], copies[1]):
        c.start()
    for b, (hg, hu, hd) in enumerate(((wg_ref, wu_ref, wd_ref), held)):
        if b:
            for c in copies:
                c.wait()
        act = None
        for h in range(NH):
            g = g_ref[:, h, b * 32 : b * 32 + 32].reshape(HALF, PART)
            a = dot(g, hd[:, h * PART : (h + 1) * PART], ((1,), (1,)))
            act = a if act is None else act + a
        gate = (act * dgate_ref[b]).astype(BF16)
        up = (act * dup_ref[b]).astype(BF16)
        for h in range(NH):
            part = dot(gate, hg[h * PART : (h + 1) * PART, :], ((1,), (1,)))
            part = part + dot(up, hu[h * PART : (h + 1) * PART, :], ((1,), (1,)))
            out_ref[:, h, b * 32 : b * 32 + 32] = part.astype(BF16).reshape(NY, 32, PART)


def reduce_body(p_ref, out_ref):
    total = p_ref[:, 0].astype(F32)
    for h in range(1, NH):
        total = total + p_ref[:, h].astype(F32)
    row, lane = iota((ROWS, ROWS), 0), iota((ROWS, ROWS), 1)
    order = one_hot(lane == ((row >> 1) & 7) * 32 + (row >> 4) * 2 + (row & 1))
    moved = dot(order, total.astype(BF16).reshape(ROWS, PART)).astype(BF16)
    out_ref[...] = moved.reshape(NZ, 16, PART)


def spread_body(r_ref, out_ref):
    row, lane = iota((ROWS, ROWS), 0), iota((ROWS, ROWS), 1)
    order = one_hot(lane == ((row >> 1) & 15) * 16 + (row >> 5) * 2 + (row & 1))
    moved = dot(order, r_ref[...].reshape(ROWS, PART)).astype(BF16).reshape(NY, 64, PART)
    for h in range(NH):
        out_ref[:, h] = moved


def gram_body(r_ref, pm_ref, share_ref, out_ref, gram_ref, layer_ref):
    out = dot(pm_ref[...], r_ref[...].reshape(ROWS, PART)).astype(BF16)
    full = dot(out, out, ((1,), (1,)))
    full = jnp.where((iota((PAIRS, PAIRS), 0) >> 3) == (iota((PAIRS, PAIRS), 1) >> 3), full, 0.0)
    packed = jnp.sum(full.reshape(TOK, TOPK, PAIRS), axis=0)
    for h in range(NH):
        gram_ref[h] = packed
    out_ref[...] = out
    layer_ref[...] = dot(share_ref[...], out.astype(F32), precision=HIGHEST).astype(BF16)


def grad_body(gram_ref, out_ref, su_ref, mask_ref, pm_ref, rows_ref):
    packed = (gram_ref[0] + gram_ref[1]) + (gram_ref[2] + gram_ref[3])
    full = jnp.broadcast_to(packed[None], (TOK, TOPK, PAIRS)).reshape(PAIRS, PAIRS)
    grad = su_ref[...] + dot(full * mask_ref[...], out_ref[...].astype(F32), precision=HIGHEST)
    rows = dot(pm_ref[...], grad.astype(BF16), ((0,), (0,))).astype(BF16)
    rows_ref[...] = rows.reshape(NZ, 16, PART)


def combine_body(r_ref, pm_ref, out_ref):
    repeat = one_hot(iota((TOK, PAIRS), 0) == (iota((TOK, PAIRS), 1) >> 3))
    pick = dot(repeat, pm_ref[...]).astype(BF16)
    out_ref[...] = dot(pick, r_ref[...].reshape(ROWS, PART)).astype(BF16)


def over_z(x):
    return lax.all_to_all(x, "z", 0, 0, tiled=True)


def over_plane(x):
    shape = x.shape
    return lax.all_to_all(x.reshape(NY * NH, 64, PART), ("y", "h"), 0, 0, tiled=True).reshape(shape)


def shards(tokens, upstream, expert_ids, gate_probs, pad_mask, gate_weight, up_weight, down_weight):
    own = [gate_weight[0], up_weight[0], down_weight[0]]
    plane = ((NY, NH, 64, PART), BF16)
    ring = ((NZ, 16, PART), BF16)
    hidden = ((2, HALF, own[0].shape[1]), F32)
    ids, probs = expert_ids.T, gate_probs.T
    where = jnp.stack([lax.axis_index("z"), lax.axis_index("c")]).astype(jnp.int32)
    (tagged,) = call(
        pack_body, [((NZ, TOK, PART + 128), BF16)], remote=(tokens, ids), space=pltpu.HBM,
        scratch=[pltpu.VMEM((TOK, PART), BF16), pltpu.VMEM((TOPK, TOK), jnp.int32), pltpu.SemaphoreType.DMA((2,))],
    )
    every = over_z(tagged)
    known = call(
        home_body,
        [((PAIRS, ROWS), BF16), ((TOK, PAIRS), F32), ((PAIRS, PART), F32), ((PAIRS, PAIRS), F32)],
        where, ids, probs, pad_mask.reshape(1, TOK), upstream, space=pltpu.VMEM,
    )
    swapped = [lax.ppermute(w, "c", [(0, 1), (1, 0)]) for w in own]
    every, known = lax.optimization_barrier((every, known))
    pm, share, su, mask = known
    (picked,) = call(select_body, [plane], where, every, space=pltpu.HBM)
    rows_in = over_plane(picked)
    held = [pltpu.VMEM(w.shape, BF16) for w in swapped]
    partial, dgate, dup = call(
        forward_body, [plane, hidden, hidden], rows_in, own[0], own[1], remote=(own[2], *swapped), space=pltpu.VMEM,
        vmem=24 << 20, scratch=[held[2], *held, pltpu.SemaphoreType.DMA((4,))],
    )
    (summed,) = call(reduce_body, [ring], over_plane(partial))
    out, gram, layer_out = call(
        gram_body,
        [((PAIRS, PART), BF16), ((NH, TOPK, PAIRS), F32), ((TOK, PART), BF16)],
        over_z(summed), pm, share,
    )
    gram = lax.all_to_all(gram, "h", 0, 0, tiled=True)
    (grad_rows,) = call(grad_body, [ring], gram, out, su, mask, pm)
    (spread,) = call(spread_body, [plane], over_z(grad_rows))
    (partial,) = call(
        backward_body, [plane], over_plane(spread), dgate, dup, *own, remote=swapped,
        vmem=24 << 20, scratch=[*held, pltpu.SemaphoreType.DMA((3,))],
    )
    (summed,) = call(reduce_body, [ring], over_plane(partial))
    (grad_tokens,) = call(combine_body, [((TOK, PART), BF16)], over_z(summed), pm)
    return (layer_out, grad_tokens)


def solution(mesh):
    fine = Mesh(mesh.devices.reshape(NY, NZ, NC, NH), ("y", "z", "c", "h"))
    expert = ("y", "z", "c")
    in_specs = (
        P(expert, "h"),
        P(expert, "h"),
        P(expert, None),
        P(expert, None),
        P(expert),
        P(expert, None, "h"),
        P(expert, None, "h"),
        P(expert, "h", None),
    )
    return jax.shard_map(shards, mesh=fine, in_specs=in_specs, out_specs=(P(expert, "h"), P(expert, "h")), check_vma=False)
```

```python
import math

import jax
import jax.numpy as jnp
from jax import lax
from jax.experimental import pallas as pl
from jax.experimental.pallas import tpu as pltpu
from jax.sharding import Mesh
from jax.sharding import PartitionSpec as P

orth_weight = 0.25
NY, NZ, NC, NH = 4, 16, 2, 4
TOK, TOPK, WIDE, PART = 16, 8, 2048, 512
PAIRS = TOK * TOPK
ROWS, HALF = 256, 128
F32, BF16 = jnp.float32, jnp.bfloat16
HIGHEST = lax.Precision.HIGHEST


def iota(shape, dim):
    return lax.broadcasted_iota(jnp.int32, shape, dim)


def one_hot(where):
    return jnp.where(where, 1.0, 0.0).astype(BF16)


def dot(a, b, dims=((1,), (0,)), precision=None):
    return lax.dot_general(a, b, (dims, ((), ())), precision=precision, preferred_element_type=F32)


def call(body, outs, *operands, vmem=8 << 20, spaces=None, remote=(), scratch=()):
    specs = [pl.BlockSpec(memory_space=pltpu.SMEM if o.ndim == 1 else pltpu.VMEM) for o in operands]
    specs += [pl.BlockSpec(memory_space=pltpu.HBM) for _ in remote]
    return pl.pallas_call(
        body,
        out_shape=[make(*out) for make, out in zip(spaces or [jax.ShapeDtypeStruct] * len(outs), outs)],
        in_specs=specs,
        out_specs=[pl.BlockSpec(memory_space=pltpu.VMEM) for _ in outs],
        scratch_shapes=scratch,
        compiler_params=pltpu.CompilerParams(vmem_limit_bytes=vmem),
    )(*operands, *(pltpu.with_memory_space_constraint(r, pltpu.HBM) for r in remote))


def owners():
    return (iota((PAIRS, TOK), 0) >> 3) == iota((PAIRS, TOK), 1)


def place_body(tok_hbm, ids_hbm, out_ref, pm_ref, tok_ref, ids_ref, sems):
    copies = [pltpu.make_async_copy(ids_hbm, ids_ref, sems.at[0]), pltpu.make_async_copy(tok_hbm, tok_ref, sems.at[1])]
    for c in copies:
        c.start()
    pair, lane = iota((PAIRS, 1), 0), iota((1, PAIRS), 1)
    repeat = one_hot(owners())
    copies[0].wait()
    ids = ids_ref[...].astype(F32).astype(BF16)
    tall = dot(repeat, ids, ((1,), (1,)))
    ids_col = jnp.sum(jnp.where(iota((PAIRS, TOPK), 1) == (pair & 7), tall, 0.0), axis=1, keepdims=True)
    flat = dot(ids, repeat, ((1,), (1,)))
    ids_row = jnp.sum(jnp.where(iota((TOPK, PAIRS), 0) == (lane & 7), flat, 0.0), axis=0, keepdims=True)
    before = (ids_col == ids_row) & ((lane >> 3) < (pair >> 3))
    slot = jnp.sum(jnp.where(before, 1.0, 0.0), axis=1, keepdims=True)
    row = iota((1, ROWS), 1)
    other = ((row >> 1) + lax.axis_index("c")) & 1
    expert = ((((row >> 2) & 3) * NZ + (row >> 4)) * NC + other).astype(F32)
    pm = one_hot((expert == ids_col) & ((row & 1).astype(F32) == slot))
    pm_ref[...] = pm
    pick = dot(pm, repeat, ((0,), (0,))).astype(BF16)
    copies[1].wait()
    out_ref[...] = dot(pick, tok_ref[...]).astype(BF16).reshape(NZ, 16, PART)


def home_body(probs_ref, pad_ref, up_ref, share_ref, su_ref, mask_ref):
    pair, lane = iota((PAIRS, 1), 0), iota((1, PAIRS), 1)
    owner = owners()
    repeat = one_hot(owner)
    pad_col = jnp.sum(jnp.where(owner, pad_ref[...].astype(F32), 0.0), axis=1, keepdims=True)
    probs = probs_ref[...]
    shares = probs / jnp.sum(probs, axis=0, keepdims=True)
    wide = repeat.astype(F32)
    share_tall = dot(wide, shares, ((1,), (1,)), HIGHEST)
    mine = iota((PAIRS, TOPK), 1) == (pair & 7)
    share_col = jnp.sum(jnp.where(mine, share_tall, 0.0), axis=1, keepdims=True)
    share_flat = dot(shares, wide, ((1,), (1,)), HIGHEST)
    share_row = jnp.sum(jnp.where(iota((TOPK, PAIRS), 0) == (lane & 7), share_flat, 0.0), axis=0, keepdims=True)
    share_ref[...] = jnp.where(iota((TOK, PAIRS), 0) == (iota((TOK, PAIRS), 1) >> 3), share_row, 0.0)
    su_ref[...] = (pad_col * share_col) * dot(repeat, up_ref[...])
    same = ((lane >> 3) == (pair >> 3)) & (lane != pair)
    mask_ref[...] = jnp.where(same, pad_col * (orth_weight / math.sqrt(WIDE)), 0.0)


def wide_rows(ref, b):
    return jnp.concatenate([ref[:, h, b * 32 : b * 32 + 32].reshape(HALF, PART) for h in range(NH)], axis=1)


def put_rows(ref, b, rows):
    for h in range(NH):
        ref[:, h, b * 32 : b * 32 + 32] = rows[:, h * PART : (h + 1) * PART].reshape(NY, 32, PART)


def forward_body(x_ref, wg_ref, wu_ref, *refs):
    hbm, (out_ref, dgate_ref, dup_ref), held, sems = refs[:4], refs[4:7], refs[7:11], refs[11]
    copies = [pltpu.make_async_copy(src, dst, sems.at[i]) for i, (src, dst) in enumerate(zip(hbm, held))]
    for c in copies:
        c.start()
    for b, (hg, hu, hd) in enumerate(((wg_ref, wu_ref, held[0]), held[1:])):
        if b:
            copies[1].wait()
            copies[2].wait()
        x = wide_rows(x_ref, b)
        gate, up = dot(x, hg[...]), dot(x, hu[...])
        sigma = 1.0 / (1.0 + jnp.exp(-gate))
        act = gate * sigma
        hidden = (act * up).astype(BF16)
        dup_ref[b] = act
        dgate_ref[b] = up * sigma * (1.0 + gate * (1.0 - sigma))
        copies[3 if b else 0].wait()
        put_rows(out_ref, b, dot(hidden, hd[...]).astype(BF16))


def backward_body(g_ref, dgate_ref, dup_ref, *refs):
    out_ref = refs[6]
    for b, (hg, hu, hd) in enumerate((refs[0:3], refs[3:6])):
        act = dot(wide_rows(g_ref, b), hd[...], ((1,), (1,)))
        gate, up = (act * dgate_ref[b]).astype(BF16), (act * dup_ref[b]).astype(BF16)
        rows = dot(gate, hg[...], ((1,), (1,))) + dot(up, hu[...], ((1,), (1,)))
        put_rows(out_ref, b, rows.astype(BF16))


def reduce_body(p_ref, out_ref):
    total = p_ref[:, 0].astype(F32)
    for h in range(1, NH):
        total = total + p_ref[:, h].astype(F32)
    row, lane = iota((ROWS, ROWS), 0), iota((ROWS, ROWS), 1)
    order = one_hot(lane == ((row >> 1) & 7) * 32 + (row >> 4) * 2 + (row & 1))
    moved = dot(order, total.astype(BF16).reshape(ROWS, PART)).astype(BF16)
    out_ref[...] = moved.reshape(NZ, 16, PART)


def spread_body(r_ref, out_ref):
    row, lane = iota((ROWS, ROWS), 0), iota((ROWS, ROWS), 1)
    order = one_hot(lane == ((row >> 1) & 15) * 16 + (row >> 5) * 2 + (row & 1))
    moved = dot(order, r_ref[...].reshape(ROWS, PART)).astype(BF16).reshape(NY, 64, PART)
    for h in range(NH):
        out_ref[:, h] = moved


def gram_body(r_ref, pm_ref, share_ref, out_ref, gram_ref, layer_ref):
    out = dot(pm_ref[...], r_ref[...].reshape(ROWS, PART)).astype(BF16)
    full = dot(out, out, ((1,), (1,)))
    full = jnp.where((iota((PAIRS, PAIRS), 0) >> 3) == (iota((PAIRS, PAIRS), 1) >> 3), full, 0.0)
    packed = jnp.sum(full.reshape(TOK, TOPK, PAIRS), axis=0)
    for h in range(NH):
        gram_ref[h] = packed
    out_ref[...] = out
    layer_ref[...] = dot(share_ref[...], out.astype(F32), precision=HIGHEST).astype(BF16)


def grad_body(gram_ref, out_ref, su_ref, mask_ref, pm_ref, rows_ref):
    packed = (gram_ref[0] + gram_ref[1]) + (gram_ref[2] + gram_ref[3])
    full = jnp.broadcast_to(packed[None], (TOK, TOPK, PAIRS)).reshape(PAIRS, PAIRS)
    grad = su_ref[...] + dot(full * mask_ref[...], out_ref[...].astype(F32), precision=HIGHEST)
    rows = dot(pm_ref[...], grad.astype(BF16), ((0,), (0,))).astype(BF16)
    rows_ref[...] = rows.reshape(NZ, 16, PART)


def combine_body(r_ref, pm_ref, out_ref):
    repeat = one_hot(iota((TOK, PAIRS), 0) == (iota((TOK, PAIRS), 1) >> 3))
    pick = dot(repeat, pm_ref[...]).astype(BF16)
    out_ref[...] = dot(pick, r_ref[...].reshape(ROWS, PART)).astype(BF16)


def over_z(x):
    return lax.all_to_all(x, "z", 0, 0, tiled=True)


def over_plane(x):
    shape = x.shape
    return lax.all_to_all(x.reshape(NY * NH, 64, PART), ("y", "h"), 0, 0, tiled=True).reshape(shape)


def shards(tokens, upstream, expert_ids, gate_probs, pad_mask, gate_weight, up_weight, down_weight):
    own = [gate_weight[0], up_weight[0], down_weight[0]]
    plane = ((NY, NH, 64, PART), BF16)
    ring = ((NZ, 16, PART), BF16)
    hidden = ((2, HALF, own[0].shape[1]), F32)
    placed, pm = call(
        place_body, [ring, ((PAIRS, ROWS), BF16)], remote=(tokens, expert_ids.T), spaces=(pltpu.HBM, pltpu.VMEM),
        scratch=[pltpu.VMEM((TOK, PART), BF16), pltpu.VMEM((TOPK, TOK), jnp.int32), pltpu.SemaphoreType.DMA((2,))],
    )
    rows = over_z(placed)
    swapped = [lax.ppermute(w, "c", [(0, 1), (1, 0)]) for w in own]
    known = call(
        home_body,
        [((TOK, PAIRS), F32), ((PAIRS, PART), F32), ((PAIRS, PAIRS), F32)],
        gate_probs.T, pad_mask.reshape(1, TOK), upstream, spaces=(pltpu.VMEM,) * 3,
    )
    rows, (share, su, mask) = lax.optimization_barrier((rows, known))
    (spread,) = call(spread_body, [plane], rows, spaces=(pltpu.HBM,))
    rows_in = over_plane(spread)
    late = [own[2], *swapped]
    partial, dgate, dup, *late = call(
        forward_body, [plane, hidden, hidden, *((w.shape, BF16) for w in late)], rows_in, own[0], own[1],
        remote=late, spaces=(pltpu.VMEM,) * 7, vmem=24 << 20, scratch=[pltpu.SemaphoreType.DMA((4,))],
    )
    (summed,) = call(reduce_body, [ring], over_plane(partial))
    out, gram, layer_out = call(
        gram_body,
        [((PAIRS, PART), BF16), ((NH, TOPK, PAIRS), F32), ((TOK, PART), BF16)],
        over_z(summed), pm, share,
    )
    gram = lax.all_to_all(gram, "h", 0, 0, tiled=True)
    (grad_rows,) = call(grad_body, [ring], gram, out, su, mask, pm)
    (spread,) = call(spread_body, [plane], over_z(grad_rows))
    (partial,) = call(
        backward_body, [plane], over_plane(spread), dgate, dup, own[0], own[1], *late, vmem=24 << 20,
    )
    (summed,) = call(reduce_body, [ring], over_plane(partial))
    (grad_tokens,) = call(combine_body, [((TOK, PART), BF16)], over_z(summed), pm)
    return (layer_out, grad_tokens)


def solution(mesh):
    fine = Mesh(mesh.devices.reshape(NY, NZ, NC, NH), ("y", "z", "c", "h"))
    expert = ("y", "z", "c")
    in_specs = (
        P(expert, "h"),
        P(expert, "h"),
        P(expert, None),
        P(expert, None),
        P(expert),
        P(expert, None, "h"),
        P(expert, None, "h"),
        P(expert, "h", None),
    )
    return jax.shard_map(shards, mesh=fine, in_specs=in_specs, out_specs=(P(expert, "h"), P(expert, "h")), check_vma=False)
```

```python
import math

import jax
import jax.numpy as jnp
from jax import lax
from jax.experimental import pallas as pl
from jax.experimental.pallas import tpu as pltpu
from jax.sharding import Mesh
from jax.sharding import PartitionSpec as P

orth_weight = 0.25
NY, NZ, NC, NH = 4, 16, 2, 4
TOK, TOPK, WIDE, PART = 16, 8, 2048, 512
PAIRS = TOK * TOPK
ROWS, HALF, PIECES = 256, 128, 4
F32, BF16 = jnp.float32, jnp.bfloat16
HIGHEST = lax.Precision.HIGHEST


def iota(shape, dim):
    return lax.broadcasted_iota(jnp.int32, shape, dim)


def one_hot(where):
    return jnp.where(where, 1.0, 0.0).astype(BF16)


def dot(a, b, dims=((1,), (0,)), precision=None):
    return lax.dot_general(a, b, (dims, ((), ())), precision=precision, preferred_element_type=F32)


def fine_dot(a, b):
    high = a.astype(BF16)
    return dot(high, b) + dot((a - high.astype(F32)).astype(BF16), b)


def call(body, outs, *operands, vmem=8 << 20, spaces=None, remote=(), scratch=()):
    specs = [pl.BlockSpec(memory_space=pltpu.SMEM if o.ndim == 1 else pltpu.VMEM) for o in operands]
    specs += [pl.BlockSpec(memory_space=pltpu.HBM) for _ in remote]
    return pl.pallas_call(
        body,
        out_shape=[make(*out) for make, out in zip(spaces or [jax.ShapeDtypeStruct] * len(outs), outs)],
        in_specs=specs,
        out_specs=[pl.BlockSpec(memory_space=pltpu.HBM if body is spread_out_body else pltpu.VMEM) for _ in outs],
        scratch_shapes=scratch,
        compiler_params=pltpu.CompilerParams(vmem_limit_bytes=vmem),
    )(*operands, *(pltpu.with_memory_space_constraint(r, pltpu.HBM) for r in remote))


def owners():
    return (iota((PAIRS, TOK), 0) >> 3) == iota((PAIRS, TOK), 1)


def place_body(tok_hbm, ids_hbm, out_ref, pm_ref, tok_ref, ids_ref, sems):
    copies = [pltpu.make_async_copy(ids_hbm, ids_ref, sems.at[0]), pltpu.make_async_copy(tok_hbm, tok_ref, sems.at[1])]
    for c in copies:
        c.start()
    pair, lane = iota((PAIRS, 1), 0), iota((1, PAIRS), 1)
    repeat = one_hot(owners())
    copies[0].wait()
    ids = ids_ref[...].astype(F32).astype(BF16)
    tall = dot(repeat, ids, ((1,), (1,)))
    ids_col = jnp.sum(jnp.where(iota((PAIRS, TOPK), 1) == (pair & 7), tall, 0.0), axis=1, keepdims=True)
    flat = dot(ids, repeat, ((1,), (1,)))
    ids_row = jnp.sum(jnp.where(iota((TOPK, PAIRS), 0) == (lane & 7), flat, 0.0), axis=0, keepdims=True)
    before = (ids_col == ids_row) & ((lane >> 3) < (pair >> 3))
    slot = jnp.sum(jnp.where(before, 1.0, 0.0), axis=1, keepdims=True)
    row = iota((1, ROWS), 1)
    other = ((row >> 1) + lax.axis_index("c")) & 1
    expert = ((((row >> 2) & 3) * NZ + (row >> 4)) * NC + other).astype(F32)
    pm = one_hot((expert == ids_col) & ((row & 1).astype(F32) == slot))
    pm_ref[...] = pm
    pick = dot(pm, repeat, ((0,), (0,))).astype(BF16)
    copies[1].wait()
    out_ref[...] = dot(pick, tok_ref[...]).astype(BF16).reshape(NZ, 16, PART)


def home_body(probs_ref, pad_ref, up_ref, share_ref, su_ref, mask_ref):
    pair, lane = iota((PAIRS, 1), 0), iota((1, PAIRS), 1)
    owner = owners()
    repeat = one_hot(owner)
    pad_col = jnp.sum(jnp.where(owner, pad_ref[...].astype(F32), 0.0), axis=1, keepdims=True)
    probs = probs_ref[...]
    shares = probs / jnp.sum(probs, axis=0, keepdims=True)
    wide = repeat.astype(F32)
    share_tall = dot(wide, shares, ((1,), (1,)), HIGHEST)
    mine = iota((PAIRS, TOPK), 1) == (pair & 7)
    share_col = jnp.sum(jnp.where(mine, share_tall, 0.0), axis=1, keepdims=True)
    share_flat = dot(shares, wide, ((1,), (1,)), HIGHEST)
    share_row = jnp.sum(jnp.where(iota((TOPK, PAIRS), 0) == (lane & 7), share_flat, 0.0), axis=0, keepdims=True)
    share_ref[...] = jnp.where(iota((TOK, PAIRS), 0) == (iota((TOK, PAIRS), 1) >> 3), share_row, 0.0)
    su_ref[...] = (pad_col * share_col) * dot(repeat, up_ref[...])
    same = ((lane >> 3) == (pair >> 3)) & (lane != pair)
    mask_ref[...] = jnp.where(same, pad_col * (orth_weight / math.sqrt(WIDE)), 0.0)


def wide_rows(ref, b):
    return jnp.concatenate([ref[:, h, b * 32 : b * 32 + 32].reshape(HALF, PART) for h in range(NH)], axis=1)


def put_rows(ref, b, rows):
    for h in range(NH):
        ref[:, h, b * 32 : b * 32 + 32] = rows[:, h * PART : (h + 1) * PART].reshape(NY, 32, PART)


def start(copies):
    for c in copies:
        c.start()


def wait(copies):
    for c in copies:
        c.wait()


def forward_body(wg_ref, wu_ref, x_hbm, *refs):
    hbm, (out_ref, dgate_ref, dup_ref), held, (x_ref, sems) = refs[:4], refs[4:7], refs[7:11], refs[11:]
    def parts(i):
        rows = hbm[i].shape[0] // PIECES
        return [
            pltpu.make_async_copy(hbm[i].at[p * rows : (p + 1) * rows], held[i].at[p * rows : (p + 1) * rows], sems.at[i, p])
            for p in range(PIECES)
        ]

    copies = [parts(i) for i in range(4)]
    inputs = [pltpu.make_async_copy(x_hbm.at[:, h], x_ref.at[:, h], sems.at[4, h]) for h in range(NH)]
    for group in (inputs, *copies):
        start(group)
    wait(inputs)
    for b, (hg, hu, hd) in enumerate(((wg_ref, wu_ref, held[0]), held[1:])):
        if b:
            wait(copies[1] + copies[2])
        x = wide_rows(x_ref, b)
        gate, up = dot(x, hg[...]), dot(x, hu[...])
        sigma = 1.0 / (1.0 + jnp.exp(-gate))
        act = gate * sigma
        hidden = (act * up).astype(BF16)
        dup_ref[b] = act
        dgate_ref[b] = up * sigma * (1.0 + gate * (1.0 - sigma))
        wait(copies[3 if b else 0])
        put_rows(out_ref, b, dot(hidden, hd[...]).astype(BF16))


def backward_body(g_ref, dgate_ref, dup_ref, *refs):
    out_ref = refs[6]
    for b, (hg, hu, hd) in enumerate((refs[0:3], refs[3:6])):
        act = dot(wide_rows(g_ref, b), hd[...], ((1,), (1,)))
        gate, up = (act * dgate_ref[b]).astype(BF16), (act * dup_ref[b]).astype(BF16)
        rows = dot(gate, hg[...], ((1,), (1,))) + dot(up, hu[...], ((1,), (1,)))
        put_rows(out_ref, b, rows.astype(BF16))


def reduce_body(p_ref, out_ref):
    total = p_ref[:, 0].astype(F32)
    for h in range(1, NH):
        total = total + p_ref[:, h].astype(F32)
    row, lane = iota((ROWS, ROWS), 0), iota((ROWS, ROWS), 1)
    order = one_hot(lane == ((row >> 1) & 7) * 32 + (row >> 4) * 2 + (row & 1))
    moved = dot(order, total.astype(BF16).reshape(ROWS, PART)).astype(BF16)
    out_ref[...] = moved.reshape(NZ, 16, PART)


def spread_body(r_ref, out_ref):
    row, lane = iota((ROWS, ROWS), 0), iota((ROWS, ROWS), 1)
    order = one_hot(lane == ((row >> 1) & 15) * 16 + (row >> 5) * 2 + (row & 1))
    moved = dot(order, r_ref[...].reshape(ROWS, PART)).astype(BF16).reshape(NY, 64, PART)
    for h in range(NH):
        out_ref[:, h] = moved


def spread_out_body(r_ref, out_hbm, moved_ref, sems):
    row, lane = iota((ROWS, ROWS), 0), iota((ROWS, ROWS), 1)
    order = one_hot(lane == ((row >> 1) & 15) * 16 + (row >> 5) * 2 + (row & 1))
    moved_ref[...] = dot(order, r_ref[...].reshape(ROWS, PART)).astype(BF16).reshape(NY, 64, PART)
    copies = [pltpu.make_async_copy(moved_ref, out_hbm.at[:, h], sems.at[h]) for h in range(NH)]
    for c in copies:
        c.start()
    for c in copies:
        c.wait()


def gram_body(r_ref, pm_ref, share_ref, out_ref, gram_ref, layer_ref):
    out = dot(pm_ref[...], r_ref[...].reshape(ROWS, PART)).astype(BF16)
    full = dot(out, out, ((1,), (1,)))
    full = jnp.where((iota((PAIRS, PAIRS), 0) >> 3) == (iota((PAIRS, PAIRS), 1) >> 3), full, 0.0)
    packed = jnp.sum(full.reshape(TOK, TOPK, PAIRS), axis=0)
    for h in range(NH):
        gram_ref[h] = packed
    out_ref[...] = out
    layer_ref[...] = fine_dot(share_ref[...], out).astype(BF16)


def grad_body(gram_ref, out_ref, su_ref, mask_ref, pm_ref, rows_ref):
    packed = (gram_ref[0] + gram_ref[1]) + (gram_ref[2] + gram_ref[3])
    full = jnp.broadcast_to(packed[None], (TOK, TOPK, PAIRS)).reshape(PAIRS, PAIRS)
    grad = su_ref[...] + fine_dot(full * mask_ref[...], out_ref[...])
    rows = dot(pm_ref[...], grad.astype(BF16), ((0,), (0,))).astype(BF16)
    rows_ref[...] = rows.reshape(NZ, 16, PART)


def combine_body(r_ref, pm_ref, out_ref):
    repeat = one_hot(iota((TOK, PAIRS), 0) == (iota((TOK, PAIRS), 1) >> 3))
    pick = dot(repeat, pm_ref[...]).astype(BF16)
    out_ref[...] = dot(pick, r_ref[...].reshape(ROWS, PART)).astype(BF16)


def over_z(x):
    return lax.all_to_all(x, "z", 0, 0, tiled=True)


def over_plane(x):
    shape = x.shape
    return lax.all_to_all(x.reshape(NY * NH, 64, PART), ("y", "h"), 0, 0, tiled=True).reshape(shape)


def shards(tokens, upstream, expert_ids, gate_probs, pad_mask, gate_weight, up_weight, down_weight):
    own = [gate_weight[0], up_weight[0], down_weight[0]]
    plane = ((NY, NH, 64, PART), BF16)
    ring = ((NZ, 16, PART), BF16)
    hidden = ((2, HALF, own[0].shape[1]), F32)
    placed, pm = call(
        place_body, [ring, ((PAIRS, ROWS), BF16)], remote=(tokens, expert_ids.T), spaces=(pltpu.HBM, pltpu.VMEM),
        scratch=[pltpu.VMEM((TOK, PART), BF16), pltpu.VMEM((TOPK, TOK), jnp.int32), pltpu.SemaphoreType.DMA((2,))],
    )
    rows = over_z(placed)
    swapped = [lax.ppermute(w, "c", [(0, 1), (1, 0)]) for w in own]
    known = call(
        home_body,
        [((TOK, PAIRS), F32), ((PAIRS, PART), F32), ((PAIRS, PAIRS), F32)],
        gate_probs.T, pad_mask.reshape(1, TOK), upstream, spaces=(pltpu.VMEM,) * 3,
    )
    rows, (share, su, mask) = lax.optimization_barrier((rows, known))
    (spread,) = call(
        spread_out_body, [plane], rows, spaces=(pltpu.HBM,), scratch=[pltpu.VMEM((NY, 64, PART), BF16), pltpu.SemaphoreType.DMA((NH,))],
    )
    rows_in = over_plane(spread)
    late = [own[2], *swapped]
    partial, dgate, dup, *late = call(
        forward_body, [plane, hidden, hidden, *((w.shape, BF16) for w in late)], own[0], own[1],
        remote=(rows_in, *late), spaces=(pltpu.VMEM,) * 7, vmem=24 << 20,
        scratch=[pltpu.VMEM(*plane), pltpu.SemaphoreType.DMA((5, NH))],
    )
    (summed,) = call(reduce_body, [ring], over_plane(partial))
    out, gram, layer_out = call(
        gram_body,
        [((PAIRS, PART), BF16), ((NH, TOPK, PAIRS), F32), ((TOK, PART), BF16)],
        over_z(summed), pm, share,
    )
    gram = lax.all_to_all(gram, "h", 0, 0, tiled=True)
    (grad_rows,) = call(grad_body, [ring], gram, out, su, mask, pm)
    (spread,) = call(spread_body, [plane], over_z(grad_rows))
    (partial,) = call(
        backward_body, [plane], over_plane(spread), dgate, dup, own[0], own[1], *late, vmem=24 << 20,
    )
    (summed,) = call(reduce_body, [ring], over_plane(partial))
    (grad_tokens,) = call(combine_body, [((TOK, PART), BF16)], over_z(summed), pm)
    return (layer_out, grad_tokens)


def solution(mesh):
    fine = Mesh(mesh.devices.reshape(NY, NZ, NC, NH), ("y", "z", "c", "h"))
    expert = ("y", "z", "c")
    in_specs = (
        P(expert, "h"),
        P(expert, "h"),
        P(expert, None),
        P(expert, None),
        P(expert),
        P(expert, None, "h"),
        P(expert, None, "h"),
        P(expert, "h", None),
    )
    return jax.shard_map(shards, mesh=fine, in_specs=in_specs, out_specs=(P(expert, "h"), P(expert, "h")), check_vma=False)
```

```python
import math

import jax
import jax.numpy as jnp
from jax import lax
from jax.experimental import pallas as pl
from jax.experimental.pallas import tpu as pltpu
from jax.sharding import Mesh
from jax.sharding import PartitionSpec as P

orth_weight = 0.25
NY, NZ, NC, NH = 4, 16, 2, 4
TOK, TOPK, WIDE, PART = 16, 8, 2048, 512
PAIRS = TOK * TOPK
ROWS, HALF, PIECES = 256, 128, 4
F32, BF16 = jnp.float32, jnp.bfloat16
HIGHEST = lax.Precision.HIGHEST


def iota(shape, dim):
    return lax.broadcasted_iota(jnp.int32, shape, dim)


def one_hot(where):
    return jnp.where(where, 1.0, 0.0).astype(BF16)


def dot(a, b, dims=((1,), (0,)), precision=None):
    return lax.dot_general(a, b, (dims, ((), ())), precision=precision, preferred_element_type=F32)


def fine_dot(a, b):
    high = a.astype(BF16)
    return dot(high, b) + dot((a - high.astype(F32)).astype(BF16), b)


def call(body, outs, *operands, vmem=8 << 20, spaces=None, remote=(), scratch=()):
    specs = [pl.BlockSpec(memory_space=pltpu.SMEM if o.ndim == 1 else pltpu.VMEM) for o in operands]
    specs += [pl.BlockSpec(memory_space=pltpu.HBM) for _ in remote]
    return pl.pallas_call(
        body,
        out_shape=[make(*out) for make, out in zip(spaces or [jax.ShapeDtypeStruct] * len(outs), outs)],
        in_specs=specs,
        out_specs=[pl.BlockSpec(memory_space=pltpu.HBM if body is spread_out_body else pltpu.VMEM) for _ in outs],
        scratch_shapes=scratch,
        compiler_params=pltpu.CompilerParams(vmem_limit_bytes=vmem),
    )(*operands, *(pltpu.with_memory_space_constraint(r, pltpu.HBM) for r in remote))


def owners():
    return (iota((PAIRS, TOK), 0) >> 3) == iota((PAIRS, TOK), 1)


def place_body(tok_hbm, ids_hbm, out_ref, pm_ref, turned_ref, tok_ref, ids_ref, sems):
    copies = [pltpu.make_async_copy(ids_hbm, ids_ref, sems.at[0]), pltpu.make_async_copy(tok_hbm, tok_ref, sems.at[1])]
    for c in copies:
        c.start()
    pair, lane = iota((PAIRS, 1), 0), iota((1, PAIRS), 1)
    repeat = one_hot(owners())
    copies[0].wait()
    ids = ids_ref[...].astype(F32).astype(BF16)
    tall = dot(repeat, ids, ((1,), (1,)))
    ids_col = jnp.sum(jnp.where(iota((PAIRS, TOPK), 1) == (pair & 7), tall, 0.0), axis=1, keepdims=True)
    flat = dot(ids, repeat, ((1,), (1,)))
    ids_row = jnp.sum(jnp.where(iota((TOPK, PAIRS), 0) == (lane & 7), flat, 0.0), axis=0, keepdims=True)
    same = ids_col == ids_row
    slot_row = jnp.sum(jnp.where(same & ((pair >> 3) < (lane >> 3)), 1.0, 0.0), axis=0, keepdims=True)

    def bucket(row):
        expert = (((row >> 2) & 3) * NZ + (row >> 4)) * NC + (((row >> 1) + lax.axis_index("c")) & 1)
        return expert.astype(F32), (row & 1).astype(F32)

    expert, place = bucket(iota((ROWS, 1), 0))
    turned = one_hot((expert == ids_row) & (place == slot_row))
    turned_ref[...] = turned
    pick = dot(turned, repeat).astype(BF16)
    slot = jnp.sum(jnp.where(same & ((lane >> 3) < (pair >> 3)), 1.0, 0.0), axis=1, keepdims=True)
    expert, place = bucket(iota((1, ROWS), 1))
    pm_ref[...] = one_hot((expert == ids_col) & (place == slot))
    copies[1].wait()
    out_ref[...] = dot(pick, tok_ref[...]).astype(BF16).reshape(NZ, 16, PART)


def home_body(probs_ref, pad_ref, up_ref, pm_ref, pick_ref, share_ref, su_ref, mask_ref):
    pair, lane = iota((PAIRS, 1), 0), iota((1, PAIRS), 1)
    owner = owners()
    repeat = one_hot(owner)
    pad_col = jnp.sum(jnp.where(owner, pad_ref[...].astype(F32), 0.0), axis=1, keepdims=True)
    probs = probs_ref[...]
    shares = probs / jnp.sum(probs, axis=0, keepdims=True)
    wide = repeat.astype(F32)
    share_tall = dot(wide, shares, ((1,), (1,)), HIGHEST)
    mine = iota((PAIRS, TOPK), 1) == (pair & 7)
    share_col = jnp.sum(jnp.where(mine, share_tall, 0.0), axis=1, keepdims=True)
    share_flat = dot(shares, wide, ((1,), (1,)), HIGHEST)
    share_row = jnp.sum(jnp.where(iota((TOPK, PAIRS), 0) == (lane & 7), share_flat, 0.0), axis=0, keepdims=True)
    share_ref[...] = jnp.where(iota((TOK, PAIRS), 0) == (iota((TOK, PAIRS), 1) >> 3), share_row, 0.0)
    su_ref[...] = (pad_col * share_col) * dot(repeat, up_ref[...])
    pick_ref[...] = dot(one_hot(iota((TOK, PAIRS), 0) == (iota((TOK, PAIRS), 1) >> 3)), pm_ref[...]).astype(BF16)
    same = ((lane >> 3) == (pair >> 3)) & (lane != pair)
    mask_ref[...] = jnp.where(same, pad_col * (orth_weight / math.sqrt(WIDE)), 0.0)


def wide_rows(ref, b):
    return jnp.concatenate([ref[:, h, b * 32 : b * 32 + 32].reshape(HALF, PART) for h in range(NH)], axis=1)


def put_rows(ref, b, rows):
    for h in range(NH):
        ref[:, h, b * 32 : b * 32 + 32] = rows[:, h * PART : (h + 1) * PART].reshape(NY, 32, PART)


def start(copies):
    for c in copies:
        c.start()


def wait(copies):
    for c in copies:
        c.wait()


def forward_body(wg_ref, wu_ref, x_hbm, *refs):
    hbm, (out_ref, dgate_ref, dup_ref), held, (x_ref, sems) = refs[:4], refs[4:7], refs[7:11], refs[11:]
    def parts(i):
        rows = hbm[i].shape[0] // PIECES
        return [
            pltpu.make_async_copy(hbm[i].at[p * rows : (p + 1) * rows], held[i].at[p * rows : (p + 1) * rows], sems.at[i, p])
            for p in range(PIECES)
        ]

    copies = [parts(i) for i in range(4)]
    inputs = [pltpu.make_async_copy(x_hbm.at[:, h], x_ref.at[:, h], sems.at[4, h]) for h in range(NH)]
    for group in (inputs, *copies):
        start(group)
    wait(inputs)
    for b, (hg, hu, hd) in enumerate(((wg_ref, wu_ref, held[0]), held[1:])):
        if b:
            wait(copies[1] + copies[2])
        x = wide_rows(x_ref, b)
        gate, up = dot(x, hg[...]), dot(x, hu[...])
        sigma = 1.0 / (1.0 + jnp.exp(-gate))
        act = gate * sigma
        hidden = (act * up).astype(BF16)
        dup_ref[b] = act
        dgate_ref[b] = up * sigma * (1.0 + gate * (1.0 - sigma))
        wait(copies[3 if b else 0])
        put_rows(out_ref, b, dot(hidden, hd[...]).astype(BF16))


def backward_body(g_ref, dgate_ref, dup_ref, *refs):
    out_ref = refs[6]
    for b, (hg, hu, hd) in enumerate((refs[0:3], refs[3:6])):
        act = dot(wide_rows(g_ref, b), hd[...], ((1,), (1,)))
        gate, up = (act * dgate_ref[b]).astype(BF16), (act * dup_ref[b]).astype(BF16)
        rows = dot(gate, hg[...], ((1,), (1,))) + dot(up, hu[...], ((1,), (1,)))
        put_rows(out_ref, b, rows.astype(BF16))


def reduce_body(p_ref, out_ref):
    total = p_ref[:, 0].astype(F32)
    for h in range(1, NH):
        total = total + p_ref[:, h].astype(F32)
    row, lane = iota((ROWS, ROWS), 0), iota((ROWS, ROWS), 1)
    order = one_hot(lane == ((row >> 1) & 7) * 32 + (row >> 4) * 2 + (row & 1))
    moved = dot(order, total.astype(BF16).reshape(ROWS, PART)).astype(BF16)
    out_ref[...] = moved.reshape(NZ, 16, PART)


def spread_body(r_ref, out_ref):
    row, lane = iota((ROWS, ROWS), 0), iota((ROWS, ROWS), 1)
    order = one_hot(lane == ((row >> 1) & 15) * 16 + (row >> 5) * 2 + (row & 1))
    moved = dot(order, r_ref[...].reshape(ROWS, PART)).astype(BF16).reshape(NY, 64, PART)
    for h in range(NH):
        out_ref[:, h] = moved


def spread_out_body(r_ref, out_hbm, moved_ref, sems):
    row, lane = iota((ROWS, ROWS), 0), iota((ROWS, ROWS), 1)
    order = one_hot(lane == ((row >> 1) & 15) * 16 + (row >> 5) * 2 + (row & 1))
    moved_ref[...] = dot(order, r_ref[...].reshape(ROWS, PART)).astype(BF16).reshape(NY, 64, PART)
    copies = [pltpu.make_async_copy(moved_ref, out_hbm.at[:, h], sems.at[h]) for h in range(NH)]
    for c in copies:
        c.start()
    for c in copies:
        c.wait()


def gram_body(r_ref, pm_ref, share_ref, out_ref, gram_ref, layer_ref):
    out = dot(pm_ref[...], r_ref[...].reshape(ROWS, PART)).astype(BF16)
    full = dot(out, out, ((1,), (1,)))
    full = jnp.where((iota((PAIRS, PAIRS), 0) >> 3) == (iota((PAIRS, PAIRS), 1) >> 3), full, 0.0)
    packed = jnp.sum(full.reshape(TOK, TOPK, PAIRS), axis=0)
    for h in range(NH):
        gram_ref[h] = packed
    out_ref[...] = out
    layer_ref[...] = fine_dot(share_ref[...], out).astype(BF16)


def grad_body(gram_ref, out_ref, su_ref, mask_ref, turned_ref, rows_ref):
    packed = (gram_ref[0] + gram_ref[1]) + (gram_ref[2] + gram_ref[3])
    full = jnp.broadcast_to(packed[None], (TOK, TOPK, PAIRS)).reshape(PAIRS, PAIRS)
    grad = su_ref[...] + fine_dot(full * mask_ref[...], out_ref[...])
    rows = dot(turned_ref[...], grad.astype(BF16)).astype(BF16)
    rows_ref[...] = rows.reshape(NZ, 16, PART)


def combine_body(r_ref, pick_ref, out_ref):
    out_ref[...] = dot(pick_ref[...], r_ref[...].reshape(ROWS, PART)).astype(BF16)


def over_z(x):
    return lax.all_to_all(x, "z", 0, 0, tiled=True)


def over_plane(x):
    shape = x.shape
    return lax.all_to_all(x.reshape(NY * NH, 64, PART), ("y", "h"), 0, 0, tiled=True).reshape(shape)


def shards(tokens, upstream, expert_ids, gate_probs, pad_mask, gate_weight, up_weight, down_weight):
    own = [gate_weight[0], up_weight[0], down_weight[0]]
    plane = ((NY, NH, 64, PART), BF16)
    ring = ((NZ, 16, PART), BF16)
    hidden = ((2, HALF, own[0].shape[1]), F32)
    placed, pm, turned = call(
        place_body, [ring, ((PAIRS, ROWS), BF16), ((ROWS, PAIRS), BF16)], remote=(tokens, expert_ids.T),
        spaces=(pltpu.HBM, pltpu.VMEM, pltpu.VMEM),
        scratch=[pltpu.VMEM((TOK, PART), BF16), pltpu.VMEM((TOPK, TOK), jnp.int32), pltpu.SemaphoreType.DMA((2,))],
    )
    rows = over_z(placed)
    swapped = [lax.ppermute(w, "c", [(0, 1), (1, 0)]) for w in own]
    known = call(
        home_body,
        [((TOK, ROWS), BF16), ((TOK, PAIRS), F32), ((PAIRS, PART), F32), ((PAIRS, PAIRS), F32)],
        gate_probs.T, pad_mask.reshape(1, TOK), upstream, pm, spaces=(pltpu.VMEM,) * 4,
    )
    rows, (pick, share, su, mask) = lax.optimization_barrier((rows, known))
    (spread,) = call(
        spread_out_body, [plane], rows, spaces=(pltpu.HBM,), scratch=[pltpu.VMEM((NY, 64, PART), BF16), pltpu.SemaphoreType.DMA((NH,))],
    )
    rows_in = over_plane(spread)
    late = [own[2], *swapped]
    partial, dgate, dup, *late = call(
        forward_body, [plane, hidden, hidden, *((w.shape, BF16) for w in late)], own[0], own[1],
        remote=(rows_in, *late), spaces=(pltpu.VMEM,) * 7, vmem=24 << 20,
        scratch=[pltpu.VMEM(*plane), pltpu.SemaphoreType.DMA((5, NH))],
    )
    (summed,) = call(reduce_body, [ring], over_plane(partial))
    out, gram, layer_out = call(
        gram_body,
        [((PAIRS, PART), BF16), ((NH, TOPK, PAIRS), F32), ((TOK, PART), BF16)],
        over_z(summed), pm, share,
    )
    gram = lax.all_to_all(gram, "h", 0, 0, tiled=True)
    (grad_rows,) = call(grad_body, [ring], gram, out, su, mask, turned)
    (spread,) = call(spread_body, [plane], over_z(grad_rows))
    (partial,) = call(
        backward_body, [plane], over_plane(spread), dgate, dup, own[0], own[1], *late, vmem=24 << 20,
    )
    (summed,) = call(reduce_body, [ring], over_plane(partial))
    (grad_tokens,) = call(combine_body, [((TOK, PART), BF16)], over_z(summed), pick)
    return (layer_out, grad_tokens)


def solution(mesh):
    fine = Mesh(mesh.devices.reshape(NY, NZ, NC, NH), ("y", "z", "c", "h"))
    expert = ("y", "z", "c")
    in_specs = (
        P(expert, "h"),
        P(expert, "h"),
        P(expert, None),
        P(expert, None),
        P(expert),
        P(expert, None, "h"),
        P(expert, None, "h"),
        P(expert, "h", None),
    )
    return jax.shard_map(shards, mesh=fine, in_specs=in_specs, out_specs=(P(expert, "h"), P(expert, "h")), check_vma=False)
```
